32 devices in a mesh: group: 2 (over x), gx: 16 (over z, y, core).
Axes of the slice: x: 2, y: 2, z: 4, core: 2. Of those that a mesh axis runs over, the one named last changes fastest.
Arguments:
- value: float32 [512, 64, 256], P(('group', 'gx')), parts along dimension 0, may hold values from -6 to 6
- drift: float32 [3, 512, 64, 256], P(None, ('group', 'gx')), parts along dimension 1, may hold values from -4 to 4
- gain: float32 [3, 512, 64, 256], P(None, ('group', 'gx')), parts along dimension 1, may hold values from -1 to 1
- target: int32 [512, 64, 256], P(('group', 'gx')), parts along dimension 0, may hold values 0 or 1
- obstacle: int32 [512, 64, 256], P(('group', 'gx')), parts along dimension 0, may hold values 0 or 1
Outputs:
- value_next: float32 [512, 64, 256], P(('group', 'gx')), parts along dimension 0
The draws below stay inside these ranges and needn't reach their ends.
There are 2 independent parts, one for each index of `group`. The reference program is written for one: setup_inputs(seed, part) draws one part's arguments, and reference() takes and returns one part's arrays. A program takes and returns all parts, laid end to end along the dimension named above; each array names one. Nothing has to cross between parts.
All inputs are finite; a program needn't handle non-finite values. No bound on the sum of `target` or of `obstacle` on one device may be relied on, other than what follows from the above.
Results may differ from the reference program's by a relative error of at most 0.00002.
Values sent between devices are 32-bit elements; how exact they have to be, the bound alone decides.
No kernel may reach another device: no remote copies, remote signals or barrier semaphores. Data moves between devices by JAX's collectives and lax.ppermute only.
A program may use at most 128 MiB of HBM per device.

```python
import jax
import jax.numpy as jnp
from jax import lax

NY = 64
NZ = 256
NX = 256


def draw_drift(key, part):
    key = jax.random.fold_in(key, 11)
    key_base = jax.random.fold_in(key, 0)
    ramp = jnp.arange(NX, dtype=jnp.float32) / jnp.float32(NX - 1)
    ramp = ramp.reshape(1, NX, 1, 1)
    base = jax.random.uniform(key_base, (3, NX, NY, NZ), jnp.float32, -1.0, 1.0)
    result = base * jnp.power(3.0, ramp)
    return result.astype(jnp.float32)


def set_ends(drawn, rng, smallest, largest):
    longest = drawn.shape.index(max(drawn.shape))
    spots = []
    for shift in (0, 1):
        where = [jax.random.randint(jax.random.fold_in(rng, axis), (), 0, length) for axis, length in enumerate(drawn.shape)]
        where[longest] = (where[longest] + shift) % drawn.shape[longest]
        spots.append(tuple(where))
    return drawn.at[spots[0]].set(smallest).at[spots[1]].set(largest)


def block_scale(stream_key, extent, cuts, low, largest):
    loudness, own = 1.0, jax.random.fold_in(stream_key, 6)
    for axis_at, blocks in cuts:
        draws = jnp.exp(jax.random.uniform(jax.random.fold_in(own, axis_at), (blocks,), jnp.float32, low / len(cuts), largest / len(cuts)))
        loudness = loudness * jnp.repeat(draws, extent[axis_at] // blocks).reshape([-1 if axis == axis_at else 1 for axis in range(len(extent))])
    return loudness


def bell_draw(rng, extent, spread, limit, cuts=(), kind=jnp.bfloat16):
    level = block_scale(rng, extent, cuts, -0.22, 0.18) if cuts else 1.0
    entries = jax.random.normal(rng, extent, jnp.float32) * spread * level
    return jnp.minimum(jnp.maximum(entries, -limit), limit).astype(kind)


def setup_inputs(seed: int = 0, part: int = 0) -> dict:
    splits = jax.random.split(jax.random.key(seed), 6)
    part_keys = jax.random.split(jax.random.fold_in(splits[5], part), 6)
    value = bell_draw(part_keys[0], (NX, NY, NZ), 1.0, 6.0, ((0, 16),), jnp.float32)
    drift = draw_drift(jax.random.fold_in(jax.random.fold_in(splits[5], part), 71), part)
    gain = jnp.clip(jax.random.uniform(part_keys[2], (3, NX, NY, NZ), jnp.float32, -1.0, 1.0) * block_scale(part_keys[2], (3, NX, NY, NZ), ((1, 16),), -0.4, 0.0), -1.0, 1.0)
    target = set_ends((jax.random.randint(part_keys[3], (NX, NY, NZ), 0, 8) < 1).astype(jnp.int32), jax.random.fold_in(part_keys[3], 1), 0, 1)
    obstacle = set_ends((jax.random.randint(part_keys[4], (NX, NY, NZ), 0, 6) < 1).astype(jnp.int32), jax.random.fold_in(part_keys[4], 1), 0, 1)
    return dict(value=value, drift=drift, gain=gain, target=target, obstacle=obstacle)


def weno(first, second, third, fourth, fifth):
    cand_a = first / 3.0 - 7.0 * second / 6.0 + 11.0 * third / 6.0
    cand_b = -second / 6.0 + 5.0 * third / 6.0 + fourth / 3.0
    cand_c = third / 3.0 + 5.0 * fourth / 6.0 - fifth / 6.0
    smooth_a = 13.0 / 12.0 * (first - 2.0 * second + third) ** 2 + 0.25 * (first - 4.0 * second + 3.0 * third) ** 2
    smooth_b = 13.0 / 12.0 * (second - 2.0 * third + fourth) ** 2 + 0.25 * (second - fourth) ** 2
    smooth_c = 13.0 / 12.0 * (third - 2.0 * fourth + fifth) ** 2 + 0.25 * (3.0 * third - 4.0 * fourth + fifth) ** 2
    weight_a = 0.1 / (1e-6 + smooth_a) ** 2
    weight_b = 0.6 / (1e-6 + smooth_b) ** 2
    weight_c = 0.3 / (1e-6 + smooth_c) ** 2
    return (weight_a * cand_a + weight_b * cand_b + weight_c * cand_c) / (weight_a + weight_b + weight_c)


def weno_pair(padded, axis):
    cells = padded.shape[axis] - 6
    diffs = jnp.diff(padded, axis=axis)

    def take(start):
        return lax.slice_in_dim(diffs, start, start + cells, axis=axis)

    minus = weno(take(0), take(1), take(2), take(3), take(4))
    plus = weno(take(5), take(4), take(3), take(2), take(1))
    return minus, plus


def hamilton(minus_list, plus_list, drift, gain):
    along = jnp.zeros_like(minus_list[0])
    control = jnp.zeros_like(minus_list[0])
    damping = jnp.zeros_like(minus_list[0])
    for comp in range(3):
        central = 0.5 * (minus_list[comp] + plus_list[comp])
        along = along + drift[comp] * central
        control = control + gain[comp] * central
        damping = damping + (jnp.abs(drift[comp]) + jnp.abs(gain[comp])) * 0.5 * (plus_list[comp] - minus_list[comp])
    return -(along + jnp.abs(control) - damping)


def constrain(field, target, obstacle):
    field = jnp.where(obstacle == 1, jnp.maximum(field, 1.0), field)
    return jnp.where(target == 1, jnp.minimum(field, -1.0), field)


def reference(value, drift, gain, target, obstacle):
    speed = jnp.sum(jnp.abs(drift) + jnp.abs(gain), axis=0)
    step_size = 0.5 / jnp.max(speed)

    def rate(field):
        pad_x = jnp.pad(field, ((3, 3), (0, 0), (0, 0)), mode="edge")
        pad_y = jnp.pad(field, ((0, 0), (3, 3), (0, 0)), mode="edge")
        pad_z = jnp.pad(field, ((0, 0), (0, 0), (3, 3)), mode="wrap")
        mx, px = weno_pair(pad_x, 0)
        my, py = weno_pair(pad_y, 1)
        mz, pz = weno_pair(pad_z, 2)
        return hamilton((mx, my, mz), (px, py, pz), drift, gain)

    first = constrain(value + step_size * rate(value), target, obstacle)
    second = constrain(0.75 * value + 0.25 * (first + step_size * rate(first)), target, obstacle)
    return constrain(value / 3.0 + 2.0 / 3.0 * (second + step_size * rate(second)), target, obstacle)
```

```python
import functools

import jax
import jax.numpy as jnp
from jax import lax
from jax.experimental import pallas as pl
from jax.experimental.pallas import tpu as pltpu
from jax.sharding import PartitionSpec as P

LANES = 128
SUB = 8
APPROX = True


def rcp(x):
    return pl.reciprocal(x, approx=APPROX)


def twice_square(s):
    return (s + s) * s


def inverse_weights(t, g, left, right):
    base = t * t * (4.0 / 3.0) + 1e-6
    h = base - g
    m = base + g
    l = h + left
    r = h + right
    return rcp(r * r), rcp(l * l), rcp(m * m * (1.0 / 6.0))


def blend(alpha, beta, gamma, far, near):
    gamma = 3.0 * gamma
    return (alpha * far + gamma * near) * rcp(alpha + beta + gamma)


def prep_kernel(drift, gain, target, obstacle, fp, fm, lo, hi, top):
    step = pl.program_id(0)
    speed = None
    for k in range(3):
        a = drift[k]
        w = jnp.abs(a) + jnp.abs(gain[k])
        fp[k] = a - w
        fm[k] = a + w
        speed = w if speed is None else speed + w
    lo[...] = jnp.where(obstacle[...] == 1, 1.0, -jnp.inf)
    hi[...] = jnp.where(target[...] == 1, -1.0, jnp.inf)
    rows, ny, nz = speed.shape
    m = jnp.max(speed, axis=0)
    m = jnp.max(m.reshape(ny // SUB, SUB, nz), axis=0)
    best = m[:, :LANES]
    for c in range(1, nz // LANES):
        best = jnp.maximum(best, m[:, c * LANES:(c + 1) * LANES])

    @pl.when(step == 0)
    def _():
        top[...] = best

    @pl.when(step > 0)
    def _():
        top[...] = jnp.maximum(top[...], best)


def prep(drift, gain, target, obstacle, block):
    _, rows, ny, nz = drift.shape
    big = pl.BlockSpec((3, block, ny, nz), lambda i: (0, i, 0, 0))
    one = pl.BlockSpec((block, ny, nz), lambda i: (i, 0, 0))
    sds = jax.ShapeDtypeStruct
    f32 = jnp.float32
    return pl.pallas_call(
        prep_kernel,
        grid=(rows // block,),
        in_specs=[big, big, one, one],
        out_specs=[big, big, one, one, pl.BlockSpec((SUB, LANES), lambda i: (0, 0))],
        out_shape=[sds(drift.shape, f32)] * 2 + [sds(target.shape, f32)] * 2 + [sds((SUB, LANES), f32)],
        compiler_params=pltpu.CompilerParams(vmem_limit_bytes=32 << 20),
    )(drift, gain, target, obstacle)


def fill(pad, row, value, ny, halves):
    for h in range(halves):
        part = value[:, h * LANES:(h + 1) * LANES]
        pad[row, h, SUB:SUB + ny] = part
        pad[row, h, 0:SUB] = jnp.broadcast_to(part[0:1], (SUB, LANES))
        pad[row, h, SUB + ny:2 * SUB + ny] = jnp.broadcast_to(part[ny - 1:ny], (SUB, LANES))


def x_pass(pad, fp, fm, gain, ac, bb, rows, ny, halves):
    tiles = ny // SUB

    def body(i, _):
        h = i // tiles
        y = pl.multiple_of((i % tiles) * SUB, SUB)
        u = lambda r: pad[r, h, pl.ds(y + SUB, SUB), :]
        z = pl.multiple_of(h * LANES, LANES)
        d, s, p, t, q, q2, ir, il, im = ({} for _ in range(9))
        prev = u(0)
        for r in range(rows + 5):
            nxt = u(r + 1)
            d[r] = nxt - prev
            prev = nxt
            if r >= 1:
                s[r] = d[r] - d[r - 1]
                p[r] = twice_square(s[r])
            if r >= 2:
                k = r - 1
                t[k] = s[k + 1] - s[k]
                ir[k], il[k], im[k] = inverse_weights(t[k], s[k] * s[k + 1], p[k], p[k + 1])
                if k >= 2:
                    q[k] = t[k] - t[k - 1]
                    q2[k] = q[k] + q[k]
                c = k - 1
                if c >= 3:
                    minus = blend(ir[c - 2], im[c - 1], il[c], q2[c - 1], q[c])
                    plus = blend(il[c + 1], im[c], ir[c - 1], q2[c + 1], q[c])
                    mid = 3.0 * (d[c] + d[c - 1])
                    dm = mid - t[c - 1] - minus
                    dp = mid - t[c] + plus
                    x = c - 3
                    f = lambda a: a[0, x, pl.ds(y, SUB), pl.ds(z, LANES)]
                    ac[x, h, pl.ds(y, SUB), :] = f(fp) * dp + f(fm) * dm
                    bb[x, h, pl.ds(y, SUB), :] = f(gain) * (dp + dm)
        return 0

    lax.fori_loop(0, tiles * halves, body, 0)


def roll(parts, shift, lane):
    n = len(parts)
    turned = [pltpu.roll(v, shift % LANES, 1) for v in parts]
    if shift > 0:
        return [jnp.where(lane < shift, turned[(i - 1) % n], turned[i]) for i in range(n)]
    return [jnp.where(lane >= LANES + shift, turned[(i + 1) % n], turned[i]) for i in range(n)]


def each(f, *lists):
    return [f(*a) for a in zip(*lists)]


def z_part(u, lane):
    d = each(lambda a, b: a - b, roll(u, -1, lane), u)
    d1 = roll(d, 1, lane)
    s = each(lambda a, b: a - b, d, d1)
    mid = each(lambda a, b: 3.0 * (a + b), d, d1)
    s1 = roll(s, -1, lane)
    t = each(lambda a, b: a - b, s1, s)
    t1 = roll(t, 1, lane)
    q = each(lambda a, b: a - b, t, t1)
    q2 = each(lambda a: a + a, q)
    p = each(twice_square, s)
    g = each(lambda a, b: a * b, s, s1)
    base = each(lambda a: a * a * (4.0 / 3.0) + 1e-6, t)
    h = each(lambda a, b: a - b, base, g)
    im = each(lambda a, b: rcp((a + b) * (a + b) * (1.0 / 6.0)), base, g)
    il = each(lambda a, b: rcp((a + b) * (a + b)), h, p)
    ir1 = each(lambda a, b: rcp((a + b) * (a + b)), roll(h, 1, lane), p)
    minus = each(blend, roll(ir1, 1, lane), roll(im, 1, lane), il, roll(q2, 1, lane), q)
    plus = each(blend, roll(il, -1, lane), im, ir1, roll(q2, -1, lane), q)
    dm = each(lambda a, b, c: a - b - c, mid, t1, minus)
    dp = each(lambda a, b, c: a - b + c, mid, t, plus)
    return dm, dp


def y_stage(pad, x, h, work, ny):
    wt, wq, wr, wl, wm = work
    for k in range(ny // SUB + 1):
        a = 6 + SUB * k
        u0, u1, u2, u3 = (pad[x + 3, h, a + o:a + o + SUB, :] for o in (-1, 0, 1, 2))
        d0, d1, d2 = u1 - u0, u2 - u1, u3 - u2
        s0, s1 = d1 - d0, d2 - d1
        t = s1 - s0
        wt[h, a:a + SUB] = t
        r, l, m = inverse_weights(t, s0 * s1, twice_square(s0), twice_square(s1))
        wr[h, a:a + SUB] = r
        wl[h, a:a + SUB] = l
        wm[h, a:a + SUB] = m


def y_part(pad, x, h, work, tile):
    wt, wq, wr, wl, wm = work
    c = SUB + SUB * tile
    at = lambda w, o: w[h, c + o:c + o + SUB, :]
    t2, t1, t0, tn = (at(wt, o) for o in (-2, -1, 0, 1))
    q = t0 - t1
    qa = t1 - t2
    qb = tn - t0
    minus = blend(at(wr, -2), at(wm, -1), at(wl, 0), qa + qa, q)
    plus = blend(at(wl, 1), at(wm, 0), at(wr, -1), qb + qb, q)
    mid = 3.0 * (pad[x + 3, h, c + 1:c + 1 + SUB, :] - pad[x + 3, h, c - 1:c - 1 + SUB, :])
    return mid - t1 - minus, mid - t0 + plus


def yz_pass(pad, fp, fm, gain, ac, bb, work, rows, ny, halves, finish):
    tiles = ny // SUB

    def body(x, _):
        lane = lax.broadcasted_iota(jnp.int32, (SUB, LANES), 1)
        for h in range(halves):
            y_stage(pad, x, h, work, ny)
        for tile in range(tiles):
            y = tile * SUB
            u = [pad[x + 3, h, SUB + y:2 * SUB + y, :] for h in range(halves)]
            dm, dp = z_part(u, lane)
            for h in range(halves):
                ym, yp = y_part(pad, x, h, work, tile)
                f = lambda a, k: a[k, x, y:y + SUB, h * LANES:(h + 1) * LANES]
                total = ac[x, h, y:y + SUB, :] + f(fp, 1) * yp + f(fm, 1) * ym
                total = total + f(fp, 2) * dp[h] + f(fm, 2) * dm[h]
                control = bb[x, h, y:y + SUB, :] + f(gain, 1) * (yp + ym) + f(gain, 2) * (dp[h] + dm[h])
                finish(x, y, h, u[h], total + jnp.abs(control))
        return 0

    lax.fori_loop(0, rows, body, 0)


def stage_kernel(weights, first, u, below, above, ends, kappa, value, fp, fm, gain, lo, hi, out, pad, ac, bb, *work):
    rows, ny, nz = u.shape
    halves = nz // LANES
    for r in range(3):
        fill(pad, r, jnp.where(ends[0] == 1, u[0], below[r]), ny, halves)
        fill(pad, rows + 3 + r, jnp.where(ends[1] == 1, u[rows - 1], above[r]), ny, halves)

    def load(r, _):
        fill(pad, r + 3, u[r], ny, halves)
        return 0

    lax.fori_loop(0, rows, load, 0)
    x_pass(pad, fp, fm, gain, ac, bb, rows, ny, halves)

    def finish(x, y, h, mine, total):
        at = (x, slice(y, y + SUB), slice(h * LANES, (h + 1) * LANES))
        if first:
            out[at] = total
            return
        keep, take = weights
        new = keep * value[at] + take * mine - kappa[0] * total
        out[at] = jnp.minimum(jnp.maximum(new, lo[at]), hi[at])

    yz_pass(pad, fp, fm, gain, ac, bb, work, rows, ny, halves, finish)


def stage(weights, first, u, below, above, ends, kappa, value, fp, fm, gain, lo, hi):
    rows, ny, nz = u.shape
    halves = nz // LANES
    vm = pl.BlockSpec(memory_space=pltpu.VMEM)
    sm = pl.BlockSpec(memory_space=pltpu.SMEM)
    f32 = jnp.float32
    return pl.pallas_call(
        functools.partial(stage_kernel, weights, first),
        in_specs=[vm, vm, vm, sm, sm] + [vm] * 6,
        out_specs=vm,
        out_shape=jax.ShapeDtypeStruct(u.shape, f32),
        scratch_shapes=[
            pltpu.VMEM((rows + 6, halves, ny + 2 * SUB, LANES), f32),
            pltpu.VMEM((rows, halves, ny, LANES), f32),
            pltpu.VMEM((rows, halves, ny, LANES), f32),
        ] + [pltpu.VMEM((halves, ny + 2 * SUB, LANES), f32)] * 5,
        compiler_params=pltpu.CompilerParams(vmem_limit_bytes=32 << 20),
    )(u, below, above, ends, kappa, value, fp, fm, gain, lo, hi)


def neighbours(field, count):
    up = [(i, i + 1) for i in range(count - 1)]
    down = [(i + 1, i) for i in range(count - 1)]
    below = lax.ppermute(field[-3:], "gx", up)
    above = lax.ppermute(field[:3], "gx", down)
    return below, above


def shards(value, drift, gain, target, obstacle):
    count = lax.axis_size("gx")
    place = lax.axis_index("gx")
    ends = jnp.stack([place == 0, place == count - 1]).astype(jnp.int32)
    below, above = neighbours(value, count)
    fp, fm, lo, hi, top = prep(drift, gain, target, obstacle, 4)
    step = 1
    while step < count:
        top = jnp.maximum(top, lax.ppermute(top, "gx", [(i, i ^ step) for i in range(count)]))
        step *= 2
    kappa = (0.5 / jnp.max(top) / 12.0).reshape(1)
    total = stage((1.0, 0.0), True, value, below, above, ends, kappa, value, fp, fm, gain, lo, hi)
    one = jnp.minimum(jnp.maximum(value - kappa[0] * total, lo), hi)
    below, above = neighbours(one, count)
    two = stage((0.75, 0.25), False, one, below, above, ends, 0.25 * kappa, value, fp, fm, gain, lo, hi)
    below, above = neighbours(two, count)
    return stage((1 / 3, 2 / 3), False, two, below, above, ends, 2 / 3 * kappa, value, fp, fm, gain, lo, hi)


def solution(mesh):
    flat = P(("group", "gx"), None, None)
    deep = P(None, ("group", "gx"), None, None)
    return jax.shard_map(
        shards,
        mesh=mesh,
        in_specs=(flat, deep, deep, flat, flat),
        out_specs=flat,
        check_vma=False,
    )
```

```python
import functools

import jax
import jax.numpy as jnp
from jax import lax
from jax.experimental import pallas as pl
from jax.experimental.pallas import tpu as pltpu
from jax.sharding import PartitionSpec as P

LANES = 128
SUB = 8
F32 = jnp.float32
VM = pl.BlockSpec(memory_space=pltpu.VMEM)
SM = pl.BlockSpec(memory_space=pltpu.SMEM)
ANY = pl.BlockSpec(memory_space=pl.ANY)
HBM = pl.BlockSpec(memory_space=pltpu.HBM)
LIMIT = 20 << 20


def rcp(x):
    return pl.reciprocal(x, approx=True)


def twice_square(s):
    return (s + s) * s


def inverse_weights(t, g, left, right):
    base = t * t * (4.0 / 3.0) + 1e-6
    h = base - g
    m = base + g
    l = h + left
    r = h + right
    return rcp(r * r), rcp(l * l), rcp(m * m * (1.0 / 6.0))


def blend(alpha, beta, gamma, far, near):
    gamma = 3.0 * gamma
    return (alpha * far + gamma * near) * rcp(alpha + beta + gamma)


def x_pass(load, cells, span, nz, finish):
    halves = nz // LANES

    def body(i, _):
        y = pl.multiple_of((i // halves) * SUB + span[0], SUB)
        z = pl.multiple_of((i % halves) * LANES, LANES)
        d, s, p, t, q, q2, ir, il, im = ({} for _ in range(9))
        prev = load(0, y, z)
        for r in range(cells + 5):
            nxt = load(r + 1, y, z)
            d[r] = nxt - prev
            prev = nxt
            if r >= 1:
                s[r] = d[r] - d[r - 1]
                p[r] = twice_square(s[r])
            if r >= 2:
                k = r - 1
                t[k] = s[k + 1] - s[k]
                ir[k], il[k], im[k] = inverse_weights(t[k], s[k] * s[k + 1], p[k], p[k + 1])
                if k >= 2:
                    q[k] = t[k] - t[k - 1]
                    q2[k] = q[k] + q[k]
                c = k - 1
                if c >= 3:
                    minus = blend(ir[c - 2], im[c - 1], il[c], q2[c - 1], q[c])
                    plus = blend(il[c + 1], im[c], ir[c - 1], q2[c + 1], q[c])
                    mid = 3.0 * (d[c] + d[c - 1])
                    finish(c - 3, y, z, mid - t[c - 1] - minus, mid - t[c] + plus)
        return 0

    lax.fori_loop(0, (span[1] - span[0]) // SUB * halves, body, 0)


def stage_column(col, work, n):
    wt, wr, wl, wm = work
    for k in range(n // SUB + 1):
        a = 6 + SUB * k
        u0, u1, u2, u3 = (col(a + o) for o in (-1, 0, 1, 2))
        d0, d1, d2 = u1 - u0, u2 - u1, u3 - u2
        s0, s1 = d1 - d0, d2 - d1
        t = s1 - s0
        r, l, m = inverse_weights(t, s0 * s1, twice_square(s0), twice_square(s1))
        wt[a:a + SUB] = t
        wr[a:a + SUB] = r
        wl[a:a + SUB] = l
        wm[a:a + SUB] = m


def column_part(col, work, tile):
    wt, wr, wl, wm = work
    c = SUB + SUB * tile
    at = lambda w, o: w[c + o:c + o + SUB]
    t2, t1, t0, tn = (at(wt, o) for o in (-2, -1, 0, 1))
    q = t0 - t1
    qa = t1 - t2
    qb = tn - t0
    minus = blend(at(wr, -2), at(wm, -1), at(wl, 0), qa + qa, q)
    plus = blend(at(wl, 1), at(wm, 0), at(wr, -1), qb + qb, q)
    mid = 3.0 * (col(c + 1) - col(c - 1))
    return mid - t1 - minus, mid - t0 + plus


def yz_scratch(ny, nz):
    halves = nz // LANES
    return (
        [pltpu.VMEM((2, halves, ny + 2 * SUB, LANES), F32)]
        + [pltpu.VMEM((2, halves, ny + 2 * SUB, LANES), F32)] * 4
        + [pltpu.VMEM((nz + 2 * SUB, LANES), F32)] * 5
        + [pltpu.VMEM((nz, LANES), F32)] * 2
    )


def yz_pass(u, fields, ac, bb, scratch, first, last):
    fp, fm, gain = fields
    yp = scratch[0]
    ywork = scratch[1:5]
    zp = scratch[5]
    zwork = scratch[6:10]
    zm, zd = scratch[10:12]
    _, ny, nz = u.shape
    halves = nz // LANES
    tiles = ny // SUB

    def body(i, _):
        x = first + 2 * i
        for h in range(halves):
            block = u[pl.ds(x, 2), :, h * LANES:(h + 1) * LANES].reshape(2 * ny, LANES)
            zp[SUB + h * LANES:SUB + (h + 1) * LANES] = block.T
        zp[0:SUB] = zp[nz:nz + SUB]
        zp[SUB + nz:2 * SUB + nz] = zp[SUB:2 * SUB]
        for r in range(2):
            for h in range(halves):
                for tile in range(tiles):
                    yp[r, h, SUB + tile * SUB:2 * SUB + tile * SUB] = u[x + r, tile * SUB:(tile + 1) * SUB, h * LANES:(h + 1) * LANES]
                yp[r, h, 0:SUB] = jnp.broadcast_to(u[x + r, 0:1, h * LANES:(h + 1) * LANES], (SUB, LANES))
                yp[r, h, SUB + ny:2 * SUB + ny] = jnp.broadcast_to(u[x + r, ny - 1:ny, h * LANES:(h + 1) * LANES], (SUB, LANES))
        zcol = lambda o: zp[o:o + SUB]
        stage_column(zcol, zwork, nz)
        for tile in range(nz // SUB):
            m, p = column_part(zcol, zwork, tile)
            zm[tile * SUB:(tile + 1) * SUB] = m
            zd[tile * SUB:(tile + 1) * SUB] = p
        for h in range(halves):
            m = zm[h * LANES:(h + 1) * LANES].T
            p = zd[h * LANES:(h + 1) * LANES].T
            for r in range(2):
                ycol = lambda o: yp[r, h, o:o + SUB]
                work = [w.at[r, h] for w in ywork]
                stage_column(ycol, work, ny)
                for tile in range(tiles):
                    ym, yq = column_part(ycol, work, tile)
                    a = r * ny + tile * SUB
                    zmm, zpp = m[a:a + SUB], p[a:a + SUB]
                    at = (x + r, slice(tile * SUB, (tile + 1) * SUB), slice(h * LANES, (h + 1) * LANES))
                    f = lambda w, k: w[(k,) + at]
                    ac[at] = f(fp, 1) * yq + f(fm, 1) * ym + (f(fp, 2) * zpp + f(fm, 2) * zmm)
                    bb[at] = f(gain, 1) * (yq + ym) + f(gain, 2) * (zpp + zmm)
        return 0

    lax.fori_loop(0, (last - first) // 2, body, 0)


def parity():
    return lax.rem(lax.axis_index("gx"), 2)


def first_slab():
    return lax.axis_index("gx") == 0


def last_slab():
    return lax.axis_index("gx") == lax.axis_size("gx") - 1


def call(kernel, ins, outs, scratch, args, us):
    return pl.pallas_call(
        kernel,
        in_specs=ins,
        out_specs=[s for s, _ in outs],
        out_shape=[(pltpu.VMEM(shape, F32) if s is VM else jax.ShapeDtypeStruct(shape, F32)) for s, shape in outs],
        scratch_shapes=scratch,
        cost_estimate=pl.CostEstimate(flops=int(us * 1.15e9), bytes_accessed=0, transcendentals=0),
        compiler_params=pltpu.CompilerParams(vmem_limit_bytes=LIMIT),
    )(*args)


def send_rows(u, odd, near, far):
    last = u.shape[0] - 3

    def body(r, _):
        if near is not None:
            near[r] = u[(1 - odd) * last + r]
        if far is not None:
            far[r] = u[odd * last + r]
        return 0

    lax.fori_loop(0, 3, body, 0)


def prep_kernel(chunk, value, drift, gain, fp, fm, gv, vv, near, top, dv, sems, gsems, vsem):
    rows, ny, nz = value.shape
    n = rows // chunk
    moves = []
    for i in range(n):
        at = pl.ds(i * chunk, chunk)
        a = pltpu.make_async_copy(drift.at[:, at], dv.at[:, at], sems.at[i])
        b = pltpu.make_async_copy(gain.at[:, at], gv.at[:, at], gsems.at[i])
        a.start()
        b.start()
        moves.append((a, b))
    keep = pltpu.make_async_copy(value, vv, vsem.at[0])
    keep.start()
    near[3] = jnp.zeros((ny, nz), F32)
    best = jnp.zeros((SUB, LANES), F32)
    for i in range(n):
        moves[i][0].wait()
        moves[i][1].wait()

        def body(j, best):
            x = i * chunk + j // (ny // SUB)
            y = pl.multiple_of((j % (ny // SUB)) * SUB, SUB)
            for h in range(nz // LANES):
                at = (x, pl.ds(y, SUB), slice(h * LANES, (h + 1) * LANES))
                speed = None
                for k in range(3):
                    a = dv[(k,) + at]
                    w = jnp.abs(a) + jnp.abs(gv[(k,) + at])
                    fp[(k,) + at] = a - w
                    fm[(k,) + at] = a + w
                    speed = w if speed is None else speed + w
                best = jnp.maximum(best, speed)
            return best

        best = lax.fori_loop(0, chunk * (ny // SUB), body, best, unroll=4)
    top[...] = best
    near[3, :SUB, :LANES] = best
    keep.wait()
    send_rows(vv, parity(), near, None)


def merge_kernel(vv, top, near, dep, far, both):
    best = jnp.maximum(top[...], near[3, :SUB, :LANES])
    both[...] = best
    far[3] = jnp.zeros(vv.shape[1:], F32)
    far[3, :SUB, :LANES] = best
    send_rows(vv, parity(), None, far)


def bounds_kernel(dep, target, obstacle, lo, hi, tv, ov, tsems, osems):
    rows, ny, nz = lo.shape
    n = tsems.shape[0]
    chunk = rows // n
    moves = []
    for i in range(n):
        at = pl.ds(i * chunk, chunk)
        a = pltpu.make_async_copy(target.at[at], tv.at[at], tsems.at[i])
        b = pltpu.make_async_copy(obstacle.at[at], ov.at[at], osems.at[i])
        a.start()
        b.start()
        moves.append((a, b))
    for i in range(n):
        moves[i][0].wait()
        moves[i][1].wait()

        def body(x, _):
            lo[x] = jnp.where(ov[x] == 1, 1.0, -jnp.inf)
            hi[x] = jnp.where(tv[x] == 1, -1.0, jnp.inf)
            return 0

        lax.fori_loop(i * chunk, (i + 1) * chunk, body, 0)


def yz_kernel(u, fp, fm, gain, dep, ac, bb, done, *scratch):
    yz_pass(u, (fp, fm, gain), ac, bb, scratch, 0, u.shape[0])
    done[...] = jnp.zeros_like(done)


def x_all(u, near, far, fields, ac, bb, span, finish):
    rows, ny, nz = u.shape
    odd = parity() == 1
    fp, fm, gain = fields

    def load(r, y, z):
        at = (pl.ds(y, SUB), pl.ds(z, LANES))
        if r < 3:
            got = jnp.where(odd, near[(r,) + at], far[(r,) + at])
            return jnp.where(first_slab(), u[(0,) + at], got)
        if r >= rows + 3:
            r -= rows + 3
            got = jnp.where(odd, far[(r,) + at], near[(r,) + at])
            return jnp.where(last_slab(), u[(rows - 1,) + at], got)
        return u[(r - 3,) + at]

    def sums(x, y, z, dm, dp):
        at = (x, pl.ds(y, SUB), pl.ds(z, LANES))
        a = ac[at] + fp[(0,) + at] * dp + fm[(0,) + at] * dm
        b = bb[at] + gain[(0,) + at] * (dp + dm)
        finish(x, y, z, a + jnp.abs(b))

    x_pass(load, rows, span, nz, sums)


def rate_x_kernel(span, u, near, far, fp, fm, gain, ac, bb, dep, total):
    def finish(x, y, z, s):
        total[x, pl.ds(y - span[0], SUB), pl.ds(z, LANES)] = s

    x_all(u, near, far, (fp, fm, gain), ac, bb, span, finish)


def first_kernel(mine, other, value, low, high, lo, hi, u, kappa, near, far):
    best = jnp.maximum(mine[...], other[...])
    best = jnp.max(jnp.max(best, axis=0, keepdims=True), axis=1, keepdims=True)
    k = jnp.broadcast_to(0.5 / best / 12.0, (SUB, LANES))
    kappa[...] = k
    rows, ny, nz = value.shape
    half = ny // 2

    def body(x, _):
        for y in range(0, ny, SUB):
            for z in range(0, nz, LANES):
                at = (x, slice(y, y + SUB), slice(z, z + LANES))
                part, o = (low, y) if y < half else (high, y - half)
                new = value[at] - k * part[x, o:o + SUB, z:z + LANES]
                u[at] = jnp.minimum(jnp.maximum(new, lo[at]), hi[at])
        return 0

    lax.fori_loop(0, rows, body, 0)
    send_rows(u, parity(), near, far)


def updater(weights, kappa, value, u, lo, hi, out):
    keep, take = weights

    def finish(x, y, z, total):
        at = (x, pl.ds(y, SUB), pl.ds(z, LANES))
        new = keep * value[at] + take * u[at] - (take * kappa[...]) * total
        out[at] = jnp.minimum(jnp.maximum(new, lo[at]), hi[at])
    return finish


def second_kernel(weights, u, near, far, kappa, value, fp, fm, gain, lo, hi, ac, bb, out, near_out, far_out):
    _, ny, nz = u.shape
    x_all(u, near, far, (fp, fm, gain), ac, bb, (0, ny), updater(weights, kappa, value, u, lo, hi, out))
    send_rows(out, parity(), near_out, far_out)


def third_kernel(weights, u, near, far, kappa, value, fp, fm, gain, lo, hi, ac, bb, out, keep, sems):
    _, ny, nz = u.shape
    finish = updater(weights, kappa, value, u, lo, hi, keep)
    n = sems.shape[0]
    span = ny // n
    moves = []
    for i in range(n):
        x_all(u, near, far, (fp, fm, gain), ac, bb, (i * span, (i + 1) * span), finish)
        at = pl.ds(i * span, span)
        moves.append(pltpu.make_async_copy(keep.at[:, at], out.at[:, at], sems.at[i]))
        moves[-1].start()
    for m in moves:
        m.wait()


def shards(value, drift, gain, target, obstacle):
    count = lax.axis_size("gx")
    value, drift, gain, target, obstacle = (
        pltpu.with_memory_space_constraint(a, pltpu.HBM) for a in (value, drift, gain, target, obstacle))
    rows, ny, nz = value.shape
    flat, deep, tile = (rows, ny, nz), (3, rows, ny, nz), (SUB, LANES)
    ends, more = (3, ny, nz), (4, ny, nz)
    half = (rows, ny // 2, nz)
    pairs = [(i, i ^ 1) for i in range(count)]

    def links(far):
        out = [(i, (i + 2 * far - 1) % count) for i in range(1, count, 2)]
        return out + [(b, a) for a, b in out]

    def swap(x, perm):
        return lax.ppermute(x, "gx", perm)

    chunk = 2
    dma = pltpu.SemaphoreType.DMA
    fp, fm, gv, vv, near, top = call(
        functools.partial(prep_kernel, chunk),
        [HBM, HBM, HBM],
        [(VM, deep)] * 3 + [(VM, flat), (VM, more), (VM, tile)],
        [pltpu.VMEM(deep, F32)] + [dma((rows // chunk,))] * 2 + [dma((1,))],
        (value, drift, gain), 3)
    fields = (fp, fm, gv)
    work = yz_scratch(ny, nz)
    near = swap(near, pairs)
    lo, hi = call(
        bounds_kernel, [ANY, HBM, HBM], [(VM, flat)] * 2,
        [pltpu.VMEM(flat, jnp.int32)] * 2 + [dma((4,))] * 2, (top, target, obstacle), 1)
    far, top = call(merge_kernel, [VM] * 3 + [ANY], [(VM, more), (VM, tile)], [], (vv, top, near, lo), 0.1)
    far = swap(far, links(1))
    ac, bb, done = call(yz_kernel, [VM] * 4 + [ANY], [(VM, flat)] * 2 + [(VM, tile)], work, (vv,) + fields + (top,), 6)
    top = jnp.maximum(jnp.maximum(top, done), far[3, :SUB, :LANES])
    other = swap(top, pairs)

    def rate_x(span, dep):
        return call(
            functools.partial(rate_x_kernel, span), [VM] * 8 + [ANY], [(VM, half)], [],
            (vv, near, far) + fields + (ac, bb, dep), 1.7)[0]

    low = rate_x((0, ny // 2), top)
    reach = 3
    top = jnp.maximum(top, other)
    dep = top
    while reach < count // 2:
        top = jnp.maximum(top, swap(top, links(reach)))
        other = swap(top, pairs)
        reach *= 3
        if reach < count // 2:
            top = jnp.maximum(top, other)
    high = rate_x((ny // 2, ny), dep)
    u, kappa, near, far = call(
        first_kernel, [VM] * 7, [(VM, flat), (VM, tile), (VM, ends), (VM, ends)], [],
        (top, other, vv, low, high, lo, hi), 1)
    for i, weights in enumerate(((0.75, 0.25), (1 / 3, 2 / 3))):
        far = swap(far, links(1))
        near = swap(near, pairs)
        ac, bb, _ = call(yz_kernel, [VM] * 4 + [ANY], [(VM, flat)] * 2 + [(VM, tile)], work, (u,) + fields + (kappa,), 6)
        args = (u, near, far, kappa, vv) + fields + (lo, hi, ac, bb)
        if i == 0:
            u, near, far = call(
                functools.partial(second_kernel, weights), [VM] * 12,
                [(VM, flat), (VM, ends), (VM, ends)], [], args, 3)
        else:
            return call(
                functools.partial(third_kernel, weights), [VM] * 12,
                [(ANY, flat)], [pltpu.VMEM(flat, F32), dma((4,))], args, 3)[0]


def solution(mesh):
    flat = P(("group", "gx"), None, None)
    deep = P(None, ("group", "gx"), None, None)
    return jax.shard_map(
        shards,
        mesh=mesh,
        in_specs=(flat, deep, deep, flat, flat),
        out_specs=flat,
        check_vma=False,
    )
```

```python
import functools

import jax
import jax.numpy as jnp
from jax import lax
from jax.experimental import pallas as pl
from jax.experimental.pallas import tpu as pltpu
from jax.sharding import PartitionSpec as P

LANES = 128
SUB = 8
F32 = jnp.float32
VM = pl.BlockSpec(memory_space=pltpu.VMEM)
SM = pl.BlockSpec(memory_space=pltpu.SMEM)
ANY = pl.BlockSpec(memory_space=pl.ANY)
HBM = pl.BlockSpec(memory_space=pltpu.HBM)
LIMIT = 20 << 20


def rcp(x):
    return pl.reciprocal(x, approx=True)


def twice_square(s):
    return (s + s) * s


def inverse_weights(t, g, left, right):
    base = t * t * (4.0 / 3.0) + 1e-6
    h = base - g
    m = base + g
    l = h + left
    r = h + right
    return rcp(r * r), rcp(l * l), rcp(m * m * (1.0 / 6.0))


def blend(alpha, beta, gamma, far, near):
    gamma = 3.0 * gamma
    return (alpha * far + gamma * near) * rcp(alpha + beta + gamma)


def x_pass(load, cells, span, nz, finish, after=None):
    def column(y, z):
        d, s, p, t, q, q2, ir, il, im = ({} for _ in range(9))
        prev = load(0, y, z)
        for r in range(cells + 5):
            nxt = load(r + 1, y, z)
            d[r] = nxt - prev
            prev = nxt
            if r >= 1:
                s[r] = d[r] - d[r - 1]
                p[r] = twice_square(s[r])
            if r >= 2:
                k = r - 1
                t[k] = s[k + 1] - s[k]
                ir[k], il[k], im[k] = inverse_weights(t[k], s[k] * s[k + 1], p[k], p[k + 1])
                if k >= 2:
                    q[k] = t[k] - t[k - 1]
                    q2[k] = q[k] + q[k]
                c = k - 1
                if c >= 3:
                    minus = blend(ir[c - 2], im[c - 1], il[c], q2[c - 1], q[c])
                    plus = blend(il[c + 1], im[c], ir[c - 1], q2[c + 1], q[c])
                    mid = 3.0 * (d[c] + d[c - 1])
                    finish(c - 3, y, z, mid - t[c - 1] - minus, mid - t[c] + plus)

    def body(i, _):
        y = pl.multiple_of(i * SUB + span[0], SUB)
        for z in range(0, nz, LANES):
            column(y, z)
        if after is not None:
            after(i, y)
        return 0

    lax.fori_loop(0, (span[1] - span[0]) // SUB, body, 0)


ORIGIN = SUB + 2
PAD = 3 * SUB


def column_weights(col, work, n):
    wt, wr, wl, wm = work
    for k in range(n // SUB + 1):
        a = SUB + SUB * k
        u0, u1, u2, u3 = (col(a + o) for o in (-1, 0, 1, 2))
        d0, d1, d2 = u1 - u0, u2 - u1, u3 - u2
        s0, s1 = d1 - d0, d2 - d1
        t = s1 - s0
        wt[a:a + SUB] = t
        r, l, m = inverse_weights(t, s0 * s1, twice_square(s0), twice_square(s1))
        wr[a:a + SUB] = r
        wl[a:a + SUB] = l
        wm[a:a + SUB] = m


def column_part(col, work, tile):
    wt, wr, wl, wm = work
    c = ORIGIN + SUB * tile
    at = lambda w, o: w[c + o:c + o + SUB]
    t2, t1, t0, tn = (at(wt, o) for o in (-2, -1, 0, 1))
    q = t0 - t1
    qa = t1 - t2
    qb = tn - t0
    minus = blend(at(wr, -2), at(wm, -1), at(wl, 0), qa + qa, q)
    plus = blend(at(wl, 1), at(wm, 0), at(wr, -1), qb + qb, q)
    mid = 3.0 * (col(c + 1) - col(c - 1))
    return mid - t1 - minus, mid - t0 + plus


def yz_scratch(ny, nz):
    halves = nz // LANES
    vmem = lambda *shape: pltpu.VMEM(shape, F32)
    slot = [vmem(nz + PAD, LANES)] + [vmem(nz, LANES)] * 2 + [vmem(2, halves, ny, LANES)] * 2 + [vmem(halves, 2 * ny, LANES)] * 2
    return (
        [vmem(2, halves, ny + PAD, LANES)] * 5
        + [vmem(nz + PAD, LANES)] * 4
        + slot * 2
    )


def yz_pass(u, fields, ac, bb, scratch, first, last):
    fp, fm, gain = fields
    yp, ywork, zwork = scratch[0], scratch[1:5], scratch[5:9]
    slots = (scratch[9:16], scratch[16:23])
    _, ny, nz = u.shape
    halves = nz // LANES
    tiles = ny // SUB
    pairs = (last - first) // 2

    def forward(i, slot):
        zp = slot[0]
        for h in range(halves):
            block = u[pl.ds(first + 2 * i, 2), :, h * LANES:(h + 1) * LANES].reshape(2 * ny, LANES)
            zp[ORIGIN + h * LANES:ORIGIN + (h + 1) * LANES] = block.T
        zp[ORIGIN - SUB:ORIGIN] = zp[nz + ORIGIN - SUB:nz + ORIGIN]
        zp[ORIGIN + nz:ORIGIN + nz + SUB] = zp[ORIGIN:ORIGIN + SUB]
        zp[PAD - SUB + nz:PAD + nz] = zp[PAD - SUB:PAD]

    def work(i, slot):
        zp, zm, zd, ya, yb, _, _ = slot
        x = first + 2 * i
        zcol = lambda o: zp[o:o + SUB]
        column_weights(zcol, zwork, nz)
        for tile in range(nz // SUB):
            m, p = column_part(zcol, zwork, tile)
            zm[tile * SUB:(tile + 1) * SUB] = m
            zd[tile * SUB:(tile + 1) * SUB] = p
        for r in range(2):
            for h in range(halves):
                z = slice(h * LANES, (h + 1) * LANES)
                for tile in range(tiles):
                    o = ORIGIN + tile * SUB
                    yp[r, h, o:o + SUB] = u[x + r, tile * SUB:(tile + 1) * SUB, z]
                yp[r, h, ORIGIN - SUB:ORIGIN] = jnp.broadcast_to(u[x + r, 0:1, z], (SUB, LANES))
                top = jnp.broadcast_to(u[x + r, ny - 1:ny, z], (SUB, LANES))
                yp[r, h, ORIGIN + ny:ORIGIN + ny + SUB] = top
                yp[r, h, PAD - SUB + ny:PAD + ny] = top
                ycol = lambda o: yp[r, h, o:o + SUB]
                here = [w.at[r, h] for w in ywork]
                column_weights(ycol, here, ny)
                for tile in range(tiles):
                    m, p = column_part(ycol, here, tile)
                    at = (1, x + r, slice(tile * SUB, (tile + 1) * SUB), z)
                    to = (r, h, slice(tile * SUB, (tile + 1) * SUB))
                    ya[to] = fp[at] * p + fm[at] * m
                    yb[to] = gain[at] * (p + m)

    def back(slot):
        _, zm, zd, _, _, tm, td = slot
        for h in range(halves):
            tm[h] = zm[h * LANES:(h + 1) * LANES].T
            td[h] = zd[h * LANES:(h + 1) * LANES].T

    def total(i, slot):
        _, _, _, ya, yb, tm, td = slot
        x = 2 * i
        for h in range(halves):
            for r in range(2):
                for tile in range(tiles):
                    o = r * ny + tile * SUB
                    m, p = tm[h, o:o + SUB], td[h, o:o + SUB]
                    at = (x + r, slice(tile * SUB, (tile + 1) * SUB), slice(h * LANES, (h + 1) * LANES))
                    of = (2, first + x + r) + at[1:]
                    to = (r, h, slice(tile * SUB, (tile + 1) * SUB))
                    ac[at] = ya[to] + (fp[of] * p + fm[of] * m)
                    bb[at] = yb[to] + gain[of] * (p + m)

    forward(0, slots[0])

    def body(j, _):
        forward(2 * j + 1, slots[1])
        work(2 * j, slots[0])
        back(slots[0])
        total(2 * j, slots[0])
        forward(jnp.minimum(2 * j + 2, pairs - 1), slots[0])
        work(2 * j + 1, slots[1])
        back(slots[1])
        total(2 * j + 1, slots[1])
        return 0

    lax.fori_loop(0, pairs // 2, body, 0)


def parity():
    return lax.rem(lax.axis_index("gx"), 2)


def first_slab():
    return lax.axis_index("gx") == 0


def last_slab():
    return lax.axis_index("gx") == lax.axis_size("gx") - 1


def call(kernel, ins, outs, scratch, args, us):
    return pl.pallas_call(
        kernel,
        in_specs=ins,
        out_specs=[s for s, _ in outs],
        out_shape=[(pltpu.VMEM(shape, F32) if s is VM else jax.ShapeDtypeStruct(shape, F32)) for s, shape in outs],
        scratch_shapes=scratch,
        cost_estimate=pl.CostEstimate(flops=int(us * 1.15e9), bytes_accessed=0, transcendentals=0),
        compiler_params=pltpu.CompilerParams(vmem_limit_bytes=LIMIT),
    )(*args)


def send_rows(u, odd, near, far):
    last = u.shape[0] - 3

    def body(r, _):
        near[r] = u[(1 - odd) * last + r]
        far[r] = u[odd * last + r]
        return 0

    lax.fori_loop(0, 3, body, 0)


def prep_kernel(chunk, value, drift, gain, fp, fm, gv, vv, near, far, top, dv, sems, gsems, vsem):
    rows, ny, nz = value.shape
    n = rows // chunk
    moves = []
    for i in range(n):
        at = pl.ds(i * chunk, chunk)
        a = pltpu.make_async_copy(drift.at[:, at], dv.at[:, at], sems.at[i])
        b = pltpu.make_async_copy(gain.at[:, at], gv.at[:, at], gsems.at[i])
        a.start()
        b.start()
        moves.append((a, b))
    keep = pltpu.make_async_copy(value, vv, vsem.at[0])
    keep.start()
    best = jnp.zeros((SUB, LANES), F32)
    for i in range(n):
        moves[i][0].wait()
        moves[i][1].wait()

        def body(j, best):
            x = i * chunk + j // (ny // SUB)
            y = pl.multiple_of((j % (ny // SUB)) * SUB, SUB)
            for h in range(nz // LANES):
                at = (x, pl.ds(y, SUB), slice(h * LANES, (h + 1) * LANES))
                speed = None
                for k in range(3):
                    a = dv[(k,) + at]
                    w = jnp.abs(a) + jnp.abs(gv[(k,) + at])
                    fp[(k,) + at] = a - w
                    fm[(k,) + at] = a + w
                    speed = w if speed is None else speed + w
                best = jnp.maximum(best, speed)
            return best

        best = lax.fori_loop(0, chunk * (ny // SUB), body, best, unroll=4)
    top[...] = best
    keep.wait()
    send_rows(vv, parity(), near, far)


def yz_bounds_kernel(first, last, u, fp, fm, gain, dep, target, obstacle, ac, bb, done, lo, hi, tv, ov, sems, *scratch):
    a = pltpu.make_async_copy(target, tv, sems.at[0])
    b = pltpu.make_async_copy(obstacle, ov, sems.at[1])
    a.start()
    b.start()
    yz_pass(u, (fp, fm, gain), ac, bb, scratch, first, last)
    done[...] = jnp.zeros_like(done)
    a.wait()
    b.wait()

    def body(x, _):
        lo[x] = jnp.where(ov[x] == 1, 1.0, -jnp.inf)
        hi[x] = jnp.where(tv[x] == 1, -1.0, jnp.inf)
        return 0

    lax.fori_loop(0, u.shape[0], body, 0)


def yz_kernel(first, last, u, fp, fm, gain, dep, ac, bb, done, *scratch):
    yz_pass(u, (fp, fm, gain), ac, bb, scratch, first, last)
    done[...] = jnp.zeros_like(done)


def x_all(u, near, far, fields, ac, bb, span, finish, after=None):
    rows, ny, nz = u.shape
    odd = parity() == 1
    fp, fm, gain = fields

    def load(r, y, z):
        at = (pl.ds(y, SUB), pl.ds(z, LANES))
        if r < 3:
            got = jnp.where(odd, near[(r,) + at], far[(r,) + at])
            return jnp.where(first_slab(), u[(0,) + at], got)
        if r >= rows + 3:
            r -= rows + 3
            got = jnp.where(odd, far[(r,) + at], near[(r,) + at])
            return jnp.where(last_slab(), u[(rows - 1,) + at], got)
        return u[(r - 3,) + at]

    size = ac[0].shape[0]

    def part(parts, x, at):
        return parts[0][(x,) + at] if x < size else parts[1][(x - size,) + at]

    def sums(x, y, z, dm, dp):
        at = (x, pl.ds(y, SUB), pl.ds(z, LANES))
        a = part(ac, x, at[1:]) + fp[(0,) + at] * dp + fm[(0,) + at] * dm
        b = part(bb, x, at[1:]) + gain[(0,) + at] * (dp + dm)
        finish(x, y, z, a + jnp.abs(b))

    x_pass(load, rows, span, nz, sums, after)


def rate_x_kernel(u, near, far, fp, fm, gain, ac0, bb0, ac1, bb1, dep, total, done):
    done[...] = jnp.zeros_like(done)

    def finish(x, y, z, s):
        total[x, pl.ds(y, SUB), pl.ds(z, LANES)] = s

    x_all(u, near, far, (fp, fm, gain), (ac0, ac1), (bb0, bb1), (0, u.shape[1]), finish)


def first_kernel(mine, other, value, total, lo, hi, u, kappa, near, far):
    best = jnp.maximum(mine[...], other[...])
    best = jnp.max(jnp.max(best, axis=0, keepdims=True), axis=1, keepdims=True)
    k = jnp.broadcast_to(0.5 / best / 12.0, (SUB, LANES))
    kappa[...] = k
    rows, ny, nz = value.shape

    def body(x, _):
        for y in range(0, ny, SUB):
            for z in range(0, nz, LANES):
                at = (x, slice(y, y + SUB), slice(z, z + LANES))
                new = value[at] - k * total[at]
                u[at] = jnp.minimum(jnp.maximum(new, lo[at]), hi[at])
        return 0

    lax.fori_loop(0, rows, body, 0)
    send_rows(u, parity(), near, far)


def updater(weights, kappa, value, u, lo, hi, out):
    keep, take = weights

    def finish(x, y, z, total):
        at = (x, pl.ds(y, SUB), pl.ds(z, LANES))
        new = keep * value[at] + take * u[at] - (take * kappa[...]) * total
        out[at] = jnp.minimum(jnp.maximum(new, lo[at]), hi[at])
    return finish


def second_kernel(weights, u, near, far, kappa, value, fp, fm, gain, lo, hi, ac, bb, out, near_out, far_out):
    _, ny, nz = u.shape
    x_all(u, near, far, (fp, fm, gain), (ac,), (bb,), (0, ny), updater(weights, kappa, value, u, lo, hi, out))
    send_rows(out, parity(), near_out, far_out)


def third_kernel(weights, u, near, far, kappa, value, fp, fm, gain, lo, hi, ac, bb, out, keep, sems):
    _, ny, nz = u.shape

    def move(i, y):
        at = pl.ds(y, SUB)
        return pltpu.make_async_copy(keep.at[:, at], out.at[:, at], sems.at[i])

    x_all(u, near, far, (fp, fm, gain), (ac,), (bb,), (0, ny), updater(weights, kappa, value, u, lo, hi, keep),
          lambda i, y: move(i, y).start())

    def wait(i, _):
        move(i, pl.multiple_of(i * SUB, SUB)).wait()
        return 0

    lax.fori_loop(0, ny // SUB, wait, 0)


def shards(value, drift, gain, target, obstacle):
    count = lax.axis_size("gx")
    value, drift, gain, target, obstacle = (
        pltpu.with_memory_space_constraint(a, pltpu.HBM) for a in (value, drift, gain, target, obstacle))
    rows, ny, nz = value.shape
    flat, deep, tile = (rows, ny, nz), (3, rows, ny, nz), (SUB, LANES)
    ends = (3, ny, nz)
    pairs = [(i, i ^ 1) for i in range(count)]

    links = [(i, (i + 1) % count) for i in range(1, count, 2)]
    links += [(b, a) for a, b in links]
    chips = count // 2
    order = list(range(0, chips, 2)) + list(range(chips - 1 - chips % 2, 0, -2))

    def ring(reach):
        out = [(2 * order[i] + 1, 2 * order[(i + reach) % chips]) for i in range(chips)]
        return out + [(b, a) for a, b in out]

    def swap(x, perm):
        return lax.ppermute(x, "gx", perm)

    chunk = 2
    dma = pltpu.SemaphoreType.DMA
    fp, fm, gv, vv, near, far, top = call(
        functools.partial(prep_kernel, chunk),
        [HBM, HBM, HBM],
        [(VM, deep)] * 3 + [(VM, flat), (VM, ends), (VM, ends), (VM, tile)],
        [pltpu.VMEM(deep, F32)] + [dma((rows // chunk,))] * 2 + [dma((1,))],
        (value, drift, gain), 3)
    fields = (fp, fm, gv)
    work = yz_scratch(ny, nz)
    other = swap(top, pairs)
    far = swap(far, links)
    near = swap(near, pairs)

    def join(top, other, done):
        return jnp.maximum(jnp.maximum(top, other), done)

    def rate_yz(u, first, last, dep, us):
        part = (last - first, ny, nz)
        return call(functools.partial(yz_kernel, first, last), [VM] * 4 + [ANY],
                    [(VM, part)] * 2 + [(VM, tile)], work, (u,) + fields + (dep,), us)

    mid = 2 * (3 * rows // 8)
    top = jnp.maximum(top, other)
    other = swap(top, ring(1))
    ac0, bb0, done = rate_yz(vv, 0, mid, top, 4)
    top = join(top, other, done)
    other = swap(top, pairs)
    ac1, bb1, done, lo, hi = call(
        functools.partial(yz_bounds_kernel, mid, rows), [VM] * 4 + [ANY, HBM, HBM],
        [(VM, (rows - mid, ny, nz))] * 2 + [(VM, tile)] + [(VM, flat)] * 2,
        [pltpu.VMEM(flat, jnp.int32)] * 2 + [dma((2,))] + work, (vv,) + fields + (top, target, obstacle), 3)
    top = join(top, other, done)
    reach = 3
    other = swap(top, ring(reach))
    total, done = call(
        rate_x_kernel, [VM] * 10 + [ANY], [(VM, flat), (VM, tile)], [],
        (vv, near, far) + fields + (ac0, bb0, ac1, bb1, top), 2.4)
    top = join(top, other, done)
    other = swap(top, pairs)
    while 3 * reach < count // 2:
        reach *= 3
        top = jnp.maximum(top, other)
        top = jnp.maximum(top, swap(top, ring(reach)))
        other = swap(top, pairs)
    u, kappa, near, far = call(
        first_kernel, [VM] * 6, [(VM, flat), (VM, tile), (VM, ends), (VM, ends)], [],
        (top, other, vv, total, lo, hi), 1)
    for i, weights in enumerate(((0.75, 0.25), (1 / 3, 2 / 3))):
        far = swap(far, links)
        near = swap(near, pairs)
        ac, bb, _ = rate_yz(u, 0, rows, kappa, 6)
        args = (u, near, far, kappa, vv) + fields + (lo, hi, ac, bb)
        if i == 0:
            u, near, far = call(
                functools.partial(second_kernel, weights), [VM] * 12,
                [(VM, flat), (VM, ends), (VM, ends)], [], args, 3)
        else:
            return call(
                functools.partial(third_kernel, weights), [VM] * 12,
                [(ANY, flat)], [pltpu.VMEM(flat, F32), dma((ny // SUB,))], args, 3)[0]


def solution(mesh):
    flat = P(("group", "gx"), None, None)
    deep = P(None, ("group", "gx"), None, None)
    return jax.shard_map(
        shards,
        mesh=mesh,
        in_specs=(flat, deep, deep, flat, flat),
        out_specs=flat,
        check_vma=False,
    )
```

```python
import functools

import jax
import jax.numpy as jnp
from jax import lax
from jax.experimental import pallas as pl
from jax.experimental.pallas import tpu as pltpu
from jax.sharding import PartitionSpec as P

LANES = 128
SUB = 8
F32 = jnp.float32
VM = pl.BlockSpec(memory_space=pltpu.VMEM)
SM = pl.BlockSpec(memory_space=pltpu.SMEM)
ANY = pl.BlockSpec(memory_space=pl.ANY)
HBM = pl.BlockSpec(memory_space=pltpu.HBM)
LIMIT = 20 << 20


def rcp(x):
    return pl.reciprocal(x, approx=True)


def twice_square(s):
    return (s + s) * s


def inverse_weights(t, g, left, right):
    base = t * t * (4.0 / 3.0) + 1e-6
    h = base - g
    m = base + g
    l = h + left
    r = h + right
    return rcp(r * r), rcp(l * l), rcp(m * m * (1.0 / 6.0))


def inverse_weights_direct(t, s0, s1):
    base = t * t * (4.0 / 3.0) + 1e-6
    m = base + s0 * s1
    l = base + s0 * (s0 - t)
    r = base + s1 * (s1 + t)
    return rcp(r * r), rcp(l * l), rcp(m * m * (1.0 / 6.0))


def blend(alpha, beta, gamma, far, near):
    gamma = 3.0 * gamma
    return (alpha * far + gamma * near) * rcp(alpha + beta + gamma)


def x_pass(load, cells, span, nz, finish, after=None):
    def column(y, z):
        d, s, p, t, q, q2, ir, il, im = ({} for _ in range(9))
        prev = load(0, y, z)
        for r in range(cells + 5):
            nxt = load(r + 1, y, z)
            d[r] = nxt - prev
            prev = nxt
            if r >= 1:
                s[r] = d[r] - d[r - 1]
                p[r] = twice_square(s[r])
            if r >= 2:
                k = r - 1
                t[k] = s[k + 1] - s[k]
                ir[k], il[k], im[k] = inverse_weights(t[k], s[k] * s[k + 1], p[k], p[k + 1])
                if k >= 2:
                    q[k] = t[k] - t[k - 1]
                    q2[k] = q[k] + q[k]
                c = k - 1
                if c >= 3:
                    minus = blend(ir[c - 2], im[c - 1], il[c], q2[c - 1], q[c])
                    plus = blend(il[c + 1], im[c], ir[c - 1], q2[c + 1], q[c])
                    mid = 3.0 * (d[c] + d[c - 1])
                    finish(c - 3, y, z, mid - t[c - 1] - minus, mid - t[c] + plus)

    def body(i, _):
        y = pl.multiple_of(i * SUB + span[0], SUB)
        for z in range(0, nz, LANES):
            column(y, z)
        if after is not None:
            after(i, y)
        return 0

    lax.fori_loop(0, (span[1] - span[0]) // SUB, body, 0)


ORIGIN = SUB + 2
PAD = 3 * SUB


def column_weights(col, work, n):
    wt, wr, wl, wm = work
    for k in range(n // SUB + 1):
        a = SUB + SUB * k
        u0, u1, u2, u3 = (col(a + o) for o in (-1, 0, 1, 2))
        d0, d1, d2 = u1 - u0, u2 - u1, u3 - u2
        s0, s1 = d1 - d0, d2 - d1
        t = s1 - s0
        wt[a:a + SUB] = t
        r, l, m = inverse_weights_direct(t, s0, s1)
        wr[a:a + SUB] = r
        wl[a:a + SUB] = l
        wm[a:a + SUB] = m


def column_part(col, work, tile):
    wt, wr, wl, wm = work
    c = ORIGIN + SUB * tile
    at = lambda w, o: w[c + o:c + o + SUB]
    t2, t1, t0, tn = (at(wt, o) for o in (-2, -1, 0, 1))
    q = t0 - t1
    qa = t1 - t2
    qb = tn - t0
    minus = blend(at(wr, -2), at(wm, -1), at(wl, 0), qa + qa, q)
    plus = blend(at(wl, 1), at(wm, 0), at(wr, -1), qb + qb, q)
    mid = 3.0 * (col(c + 1) - col(c - 1))
    return mid - t1 - minus, mid - t0 + plus


def yz_scratch(ny, nz):
    halves = nz // LANES
    vmem = lambda *shape: pltpu.VMEM(shape, F32)
    slot = [vmem(nz + PAD, LANES)] + [vmem(nz, LANES)] * 2 + [vmem(2, halves, ny, LANES)] * 2 + [vmem(halves, 2 * ny, LANES)] * 2
    return (
        [vmem(2, halves, ny + PAD, LANES)] * 5
        + [vmem(nz + PAD, LANES)] * 4
        + slot * 2
    )


def yz_pass(u, fields, ac, bb, scratch, first, last):
    fp, fm, gain = fields
    yp, ywork, zwork = scratch[0], scratch[1:5], scratch[5:9]
    slots = (scratch[9:16], scratch[16:23])
    _, ny, nz = u.shape
    halves = nz // LANES
    tiles = ny // SUB
    pairs = (last - first) // 2

    def forward(i, slot):
        zp = slot[0]
        for h in range(halves):
            block = u[pl.ds(first + 2 * i, 2), :, h * LANES:(h + 1) * LANES].reshape(2 * ny, LANES)
            zp[ORIGIN + h * LANES:ORIGIN + (h + 1) * LANES] = block.T
        zp[ORIGIN - SUB:ORIGIN] = zp[nz + ORIGIN - SUB:nz + ORIGIN]
        zp[ORIGIN + nz:ORIGIN + nz + SUB] = zp[ORIGIN:ORIGIN + SUB]
        zp[PAD - SUB + nz:PAD + nz] = zp[PAD - SUB:PAD]

    def work(i, slot):
        zp, zm, zd, ya, yb, _, _ = slot
        x = first + 2 * i
        zcol = lambda o: zp[o:o + SUB]
        column_weights(zcol, zwork, nz)
        for tile in range(nz // SUB):
            m, p = column_part(zcol, zwork, tile)
            zm[tile * SUB:(tile + 1) * SUB] = m
            zd[tile * SUB:(tile + 1) * SUB] = p
        for r in range(2):
            for h in range(halves):
                z = slice(h * LANES, (h + 1) * LANES)
                for tile in range(tiles):
                    o = ORIGIN + tile * SUB
                    yp[r, h, o:o + SUB] = u[x + r, tile * SUB:(tile + 1) * SUB, z]
                yp[r, h, ORIGIN - SUB:ORIGIN] = jnp.broadcast_to(u[x + r, 0:1, z], (SUB, LANES))
                top = jnp.broadcast_to(u[x + r, ny - 1:ny, z], (SUB, LANES))
                yp[r, h, ORIGIN + ny:ORIGIN + ny + SUB] = top
                yp[r, h, PAD - SUB + ny:PAD + ny] = top
                ycol = lambda o: yp[r, h, o:o + SUB]
                here = [w.at[r, h] for w in ywork]
                column_weights(ycol, here, ny)
                for tile in range(tiles):
                    m, p = column_part(ycol, here, tile)
                    at = (1, x + r, slice(tile * SUB, (tile + 1) * SUB), z)
                    to = (r, h, slice(tile * SUB, (tile + 1) * SUB))
                    ya[to] = fp[at] * p + fm[at] * m
                    yb[to] = gain[at] * (p + m)

    def back(slot):
        _, zm, zd, _, _, tm, td = slot
        for h in range(halves):
            tm[h] = zm[h * LANES:(h + 1) * LANES].T
            td[h] = zd[h * LANES:(h + 1) * LANES].T

    def total(i, slot):
        _, _, _, ya, yb, tm, td = slot
        x = 2 * i
        for h in range(halves):
            for r in range(2):
                for tile in range(tiles):
                    o = r * ny + tile * SUB
                    m, p = tm[h, o:o + SUB], td[h, o:o + SUB]
                    at = (x + r, slice(tile * SUB, (tile + 1) * SUB), slice(h * LANES, (h + 1) * LANES))
                    of = (2, first + x + r) + at[1:]
                    to = (r, h, slice(tile * SUB, (tile + 1) * SUB))
                    ac[at] = ya[to] + (fp[of] * p + fm[of] * m)
                    bb[at] = yb[to] + gain[of] * (p + m)

    forward(0, slots[0])

    def body(j, _):
        forward(2 * j + 1, slots[1])
        work(2 * j, slots[0])
        back(slots[0])
        total(2 * j, slots[0])
        forward(jnp.minimum(2 * j + 2, pairs - 1), slots[0])
        work(2 * j + 1, slots[1])
        back(slots[1])
        total(2 * j + 1, slots[1])
        return 0

    lax.fori_loop(0, pairs // 2, body, 0)


def parity():
    return lax.rem(lax.axis_index("gx"), 2)


def first_slab():
    return lax.axis_index("gx") == 0


def last_slab():
    return lax.axis_index("gx") == lax.axis_size("gx") - 1


def call(kernel, ins, outs, scratch, args, us):
    return pl.pallas_call(
        kernel,
        in_specs=ins,
        out_specs=[s for s, _ in outs],
        out_shape=[(pltpu.VMEM(shape, F32) if s is VM else jax.ShapeDtypeStruct(shape, F32)) for s, shape in outs],
        scratch_shapes=scratch,
        cost_estimate=pl.CostEstimate(flops=int(us * 1.15e9), bytes_accessed=0, transcendentals=0),
        compiler_params=pltpu.CompilerParams(vmem_limit_bytes=LIMIT),
    )(*args)


def send_rows(u, odd, near, far):
    last = u.shape[0] - 3

    def body(r, _):
        near[r] = u[(1 - odd) * last + r]
        far[r] = u[odd * last + r]
        return 0

    lax.fori_loop(0, 3, body, 0)


def prep_kernel(chunk, value, drift, gain, fp, fm, gv, vv, near, far, top, dv, sems, gsems, vsem):
    rows, ny, nz = value.shape
    n = rows // chunk
    moves = []
    for i in range(n):
        at = pl.ds(i * chunk, chunk)
        a = pltpu.make_async_copy(drift.at[:, at], dv.at[:, at], sems.at[i])
        b = pltpu.make_async_copy(gain.at[:, at], gv.at[:, at], gsems.at[i])
        a.start()
        b.start()
        moves.append((a, b))
    keep = pltpu.make_async_copy(value, vv, vsem.at[0])
    keep.start()
    best = jnp.zeros((SUB, LANES), F32)
    for i in range(n):
        moves[i][0].wait()
        moves[i][1].wait()

        def body(j, best):
            x = i * chunk + j // (ny // SUB)
            y = pl.multiple_of((j % (ny // SUB)) * SUB, SUB)
            for h in range(nz // LANES):
                at = (x, pl.ds(y, SUB), slice(h * LANES, (h + 1) * LANES))
                speed = None
                for k in range(3):
                    a = dv[(k,) + at]
                    w = jnp.abs(a) + jnp.abs(gv[(k,) + at])
                    fp[(k,) + at] = a - w
                    fm[(k,) + at] = a + w
                    speed = w if speed is None else speed + w
                best = jnp.maximum(best, speed)
            return best

        best = lax.fori_loop(0, chunk * (ny // SUB), body, best, unroll=4)
    top[...] = best
    keep.wait()
    send_rows(vv, parity(), near, far)


def yz_bounds_kernel(first, last, u, fp, fm, gain, dep, target, obstacle, ac, bb, done, lo, hi, tv, ov, sems, *scratch):
    a = pltpu.make_async_copy(target, tv, sems.at[0])
    b = pltpu.make_async_copy(obstacle, ov, sems.at[1])
    a.start()
    b.start()
    yz_pass(u, (fp, fm, gain), ac, bb, scratch, first, last)
    done[...] = jnp.zeros_like(done)
    a.wait()
    b.wait()

    def body(x, _):
        lo[x] = jnp.where(ov[x] == 1, 1.0, -jnp.inf)
        hi[x] = jnp.where(tv[x] == 1, -1.0, jnp.inf)
        return 0

    lax.fori_loop(0, u.shape[0], body, 0)


def yz_kernel(first, last, u, fp, fm, gain, dep, ac, bb, done, *scratch):
    yz_pass(u, (fp, fm, gain), ac, bb, scratch, first, last)
    done[...] = jnp.zeros_like(done)


def x_all(u, near, far, fields, ac, bb, span, finish, after=None):
    rows, ny, nz = u.shape
    odd = parity() == 1
    fp, fm, gain = fields

    def load(r, y, z):
        at = (pl.ds(y, SUB), pl.ds(z, LANES))
        if r < 3:
            got = jnp.where(odd, near[(r,) + at], far[(r,) + at])
            return jnp.where(first_slab(), u[(0,) + at], got)
        if r >= rows + 3:
            r -= rows + 3
            got = jnp.where(odd, far[(r,) + at], near[(r,) + at])
            return jnp.where(last_slab(), u[(rows - 1,) + at], got)
        return u[(r - 3,) + at]

    size = ac[0].shape[0]

    def part(parts, x, at):
        return parts[0][(x,) + at] if x < size else parts[1][(x - size,) + at]

    def sums(x, y, z, dm, dp):
        at = (x, pl.ds(y, SUB), pl.ds(z, LANES))
        a = part(ac, x, at[1:]) + fp[(0,) + at] * dp + fm[(0,) + at] * dm
        b = part(bb, x, at[1:]) + gain[(0,) + at] * (dp + dm)
        finish(x, y, z, a + jnp.abs(b))

    x_pass(load, rows, span, nz, sums, after)


def rate_x_kernel(u, near, far, fp, fm, gain, ac0, bb0, ac1, bb1, dep, total, done):
    done[...] = jnp.zeros_like(done)

    def finish(x, y, z, s):
        total[x, pl.ds(y, SUB), pl.ds(z, LANES)] = s

    x_all(u, near, far, (fp, fm, gain), (ac0, ac1), (bb0, bb1), (0, u.shape[1]), finish)


def first_kernel(mine, other, value, total, lo, hi, u, kappa, near, far):
    best = jnp.maximum(mine[...], other[...])
    best = jnp.max(jnp.max(best, axis=0, keepdims=True), axis=1, keepdims=True)
    k = jnp.broadcast_to(0.5 / best / 12.0, (SUB, LANES))
    kappa[...] = k
    rows, ny, nz = value.shape

    def body(x, _):
        for y in range(0, ny, SUB):
            for z in range(0, nz, LANES):
                at = (x, slice(y, y + SUB), slice(z, z + LANES))
                new = value[at] - k * total[at]
                u[at] = jnp.minimum(jnp.maximum(new, lo[at]), hi[at])
        return 0

    lax.fori_loop(0, rows, body, 0)
    send_rows(u, parity(), near, far)


def updater(weights, kappa, value, u, lo, hi, out):
    keep, take = weights

    def finish(x, y, z, total):
        at = (x, pl.ds(y, SUB), pl.ds(z, LANES))
        new = keep * value[at] + take * u[at] - (take * kappa[...]) * total
        out[at] = jnp.minimum(jnp.maximum(new, lo[at]), hi[at])
    return finish


def second_kernel(weights, u, near, far, kappa, value, fp, fm, gain, lo, hi, ac, bb, out, near_out, far_out):
    _, ny, nz = u.shape
    x_all(u, near, far, (fp, fm, gain), (ac,), (bb,), (0, ny), updater(weights, kappa, value, u, lo, hi, out))
    send_rows(out, parity(), near_out, far_out)


def third_kernel(weights, u, near, far, kappa, value, fp, fm, gain, lo, hi, ac, bb, out, keep, sems):
    _, ny, nz = u.shape

    def move(i, y):
        at = pl.ds(y, SUB)
        return pltpu.make_async_copy(keep.at[:, at], out.at[:, at], sems.at[i])

    x_all(u, near, far, (fp, fm, gain), (ac,), (bb,), (0, ny), updater(weights, kappa, value, u, lo, hi, keep),
          lambda i, y: move(i, y).start())

    def wait(i, _):
        move(i, pl.multiple_of(i * SUB, SUB)).wait()
        return 0

    lax.fori_loop(0, ny // SUB, wait, 0)


def shards(value, drift, gain, target, obstacle):
    count = lax.axis_size("gx")
    value, drift, gain, target, obstacle = (
        pltpu.with_memory_space_constraint(a, pltpu.HBM) for a in (value, drift, gain, target, obstacle))
    rows, ny, nz = value.shape
    flat, deep, tile = (rows, ny, nz), (3, rows, ny, nz), (SUB, LANES)
    ends = (3, ny, nz)
    pairs = [(i, i ^ 1) for i in range(count)]

    links = [(i, (i + 1) % count) for i in range(1, count, 2)]
    links += [(b, a) for a, b in links]
    chips = count // 2
    order = list(range(0, chips, 2)) + list(range(chips - 1 - chips % 2, 0, -2))

    def ring(reach):
        out = [(2 * order[i] + 1, 2 * order[(i + reach) % chips]) for i in range(chips)]
        return out + [(b, a) for a, b in out]

    def swap(x, perm):
        return lax.ppermute(x, "gx", perm)

    chunk = 2
    dma = pltpu.SemaphoreType.DMA
    fp, fm, gv, vv, near, far, top = call(
        functools.partial(prep_kernel, chunk),
        [HBM, HBM, HBM],
        [(VM, deep)] * 3 + [(VM, flat), (VM, ends), (VM, ends), (VM, tile)],
        [pltpu.VMEM(deep, F32)] + [dma((rows // chunk,))] * 2 + [dma((1,))],
        (value, drift, gain), 3)
    fields = (fp, fm, gv)
    work = yz_scratch(ny, nz)
    other = swap(top, pairs)
    far = swap(far, links)
    near = swap(near, pairs)

    def join(top, other, done):
        return jnp.maximum(jnp.maximum(top, other), done)

    def rate_yz(u, first, last, dep, us):
        part = (last - first, ny, nz)
        return call(functools.partial(yz_kernel, first, last), [VM] * 4 + [ANY],
                    [(VM, part)] * 2 + [(VM, tile)], work, (u,) + fields + (dep,), us)

    mid = 2 * (3 * rows // 8)
    top = jnp.maximum(top, other)
    other = swap(top, ring(1))
    ac0, bb0, done, lo, hi = call(
        functools.partial(yz_bounds_kernel, 0, mid), [VM] * 4 + [ANY, HBM, HBM],
        [(VM, (mid, ny, nz))] * 2 + [(VM, tile)] + [(VM, flat)] * 2,
        [pltpu.VMEM(flat, jnp.int32)] * 2 + [dma((2,))] + work, (vv,) + fields + (top, target, obstacle), 4)
    top = join(top, other, done)
    other = swap(top, pairs)
    ac1, bb1, done = rate_yz(vv, mid, rows, top, 1.5)
    top = join(top, other, done)
    reach = 3
    other = swap(top, ring(reach))
    total, done = call(
        rate_x_kernel, [VM] * 10 + [ANY], [(VM, flat), (VM, tile)], [],
        (vv, near, far) + fields + (ac0, bb0, ac1, bb1, top), 2.4)
    top = join(top, other, done)
    other = swap(top, pairs)
    while 3 * reach < count // 2:
        reach *= 3
        top = jnp.maximum(top, other)
        top = jnp.maximum(top, swap(top, ring(reach)))
        other = swap(top, pairs)
    u, kappa, near, far = call(
        first_kernel, [VM] * 6, [(VM, flat), (VM, tile), (VM, ends), (VM, ends)], [],
        (top, other, vv, total, lo, hi), 1)
    for i, weights in enumerate(((0.75, 0.25), (1 / 3, 2 / 3))):
        far = swap(far, links)
        near = swap(near, pairs)
        ac, bb, _ = rate_yz(u, 0, rows, kappa, 6)
        args = (u, near, far, kappa, vv) + fields + (lo, hi, ac, bb)
        if i == 0:
            u, near, far = call(
                functools.partial(second_kernel, weights), [VM] * 12,
                [(VM, flat), (VM, ends), (VM, ends)], [], args, 3)
        else:
            return call(
                functools.partial(third_kernel, weights), [VM] * 12,
                [(ANY, flat)], [pltpu.VMEM(flat, F32), dma((ny // SUB,))], args, 3)[0]


def solution(mesh):
    flat = P(("group", "gx"), None, None)
    deep = P(None, ("group", "gx"), None, None)
    return jax.shard_map(
        shards,
        mesh=mesh,
        in_specs=(flat, deep, deep, flat, flat),
        out_specs=flat,
        check_vma=False,
    )
```

```python
import functools

import jax
import jax.numpy as jnp
from jax import lax
from jax.experimental import pallas as pl
from jax.experimental.pallas import tpu as pltpu
from jax.sharding import PartitionSpec as P

LANES = 128
SUB = 8
F32 = jnp.float32
VM = pl.BlockSpec(memory_space=pltpu.VMEM)
SM = pl.BlockSpec(memory_space=pltpu.SMEM)
ANY = pl.BlockSpec(memory_space=pl.ANY)
HBM = pl.BlockSpec(memory_space=pltpu.HBM)
LIMIT = 20 << 20


def rcp(x):
    return pl.reciprocal(x, approx=True)


def twice_square(s):
    return (s + s) * s


def inverse_weights(t, g, left, right):
    base = t * t * (4.0 / 3.0) + 1e-6
    h = base - g
    m = base + g
    l = h + left
    r = h + right
    return rcp(r * r), rcp(l * l), rcp(m * m * (1.0 / 6.0))


def inverse_weights_direct(t, s0, s1):
    base = t * t * (4.0 / 3.0) + 1e-6
    m = base + s0 * s1
    l = base + s0 * (s0 - t)
    r = base + s1 * (s1 + t)
    return rcp(r * r), rcp(l * l), rcp(m * m * (1.0 / 6.0))


def blend(alpha, beta, gamma, far, near):
    gamma = 3.0 * gamma
    return (alpha * far + gamma * near) * rcp(alpha + beta + gamma)


def x_pass(load, cells, span, nz, finish, after=None):
    def column(y, z):
        d, s, p, t, q, q2, ir, il, im = ({} for _ in range(9))
        prev = load(0, y, z)
        for r in range(cells + 5):
            nxt = load(r + 1, y, z)
            d[r] = nxt - prev
            prev = nxt
            if r >= 1:
                s[r] = d[r] - d[r - 1]
                p[r] = twice_square(s[r])
            if r >= 2:
                k = r - 1
                t[k] = s[k + 1] - s[k]
                ir[k], il[k], im[k] = inverse_weights(t[k], s[k] * s[k + 1], p[k], p[k + 1])
                if k >= 2:
                    q[k] = t[k] - t[k - 1]
                    q2[k] = q[k] + q[k]
                c = k - 1
                if c >= 3:
                    minus = blend(ir[c - 2], im[c - 1], il[c], q2[c - 1], q[c])
                    plus = blend(il[c + 1], im[c], ir[c - 1], q2[c + 1], q[c])
                    mid = 3.0 * (d[c] + d[c - 1])
                    finish(c - 3, y, z, mid - t[c - 1] - minus, mid - t[c] + plus)

    def body(i, _):
        y = pl.multiple_of(i * SUB + span[0], SUB)
        for z in range(0, nz, LANES):
            column(y, z)
        if after is not None:
            after(i, y)
        return 0

    lax.fori_loop(0, (span[1] - span[0]) // SUB, body, 0)


ORIGIN = SUB + 2
PAD = 3 * SUB


def column_weights(col, work, n):
    wt, wr, wl, wm = work
    for k in range(n // SUB + 1):
        a = SUB + SUB * k
        u0, u1, u2, u3 = (col(a + o) for o in (-1, 0, 1, 2))
        d0, d1, d2 = u1 - u0, u2 - u1, u3 - u2
        s0, s1 = d1 - d0, d2 - d1
        t = s1 - s0
        wt[a:a + SUB] = t
        r, l, m = inverse_weights_direct(t, s0, s1)
        wr[a:a + SUB] = r
        wl[a:a + SUB] = l
        wm[a:a + SUB] = m


def column_part(col, work, tile):
    wt, wr, wl, wm = work
    c = ORIGIN + SUB * tile
    at = lambda w, o: w[c + o:c + o + SUB]
    t2, t1, t0, tn = (at(wt, o) for o in (-2, -1, 0, 1))
    q = t0 - t1
    qa = t1 - t2
    qb = tn - t0
    minus = blend(at(wr, -2), at(wm, -1), at(wl, 0), qa + qa, q)
    plus = blend(at(wl, 1), at(wm, 0), at(wr, -1), qb + qb, q)
    mid = 3.0 * (col(c + 1) - col(c - 1))
    return mid - t1 - minus, mid - t0 + plus


def yz_scratch(ny, nz):
    halves = nz // LANES
    vmem = lambda *shape: pltpu.VMEM(shape, F32)
    slot = [vmem(nz + PAD, LANES)] + [vmem(nz, LANES)] * 2 + [vmem(2, halves, ny, LANES)] * 2 + [vmem(halves, 2 * ny, LANES)] * 2
    return (
        [vmem(2, halves, ny + PAD, LANES)] * 5
        + [vmem(nz + PAD, LANES)] * 4
        + slot * 2
    )


def yz_pass(u, fields, ac, bb, scratch, first, last):
    fp, fm, gain = fields
    yp, ywork, zwork = scratch[0], scratch[1:5], scratch[5:9]
    slots = (scratch[9:16], scratch[16:23])
    _, ny, nz = u.shape
    halves = nz // LANES
    tiles = ny // SUB
    pairs = (last - first) // 2

    def forward(i, slot):
        zp = slot[0]
        for h in range(halves):
            block = u[pl.ds(first + 2 * i, 2), :, h * LANES:(h + 1) * LANES].reshape(2 * ny, LANES)
            zp[ORIGIN + h * LANES:ORIGIN + (h + 1) * LANES] = block.T
        zp[ORIGIN - SUB:ORIGIN] = zp[nz + ORIGIN - SUB:nz + ORIGIN]
        zp[ORIGIN + nz:ORIGIN + nz + SUB] = zp[ORIGIN:ORIGIN + SUB]
        zp[PAD - SUB + nz:PAD + nz] = zp[PAD - SUB:PAD]

    def work(i, slot):
        zp, zm, zd, ya, yb, _, _ = slot
        x = first + 2 * i
        zcol = lambda o: zp[o:o + SUB]
        column_weights(zcol, zwork, nz)
        for tile in range(nz // SUB):
            m, p = column_part(zcol, zwork, tile)
            zm[tile * SUB:(tile + 1) * SUB] = m
            zd[tile * SUB:(tile + 1) * SUB] = p
        for r in range(2):
            for h in range(halves):
                z = slice(h * LANES, (h + 1) * LANES)
                for tile in range(tiles):
                    o = ORIGIN + tile * SUB
                    yp[r, h, o:o + SUB] = u[x + r, tile * SUB:(tile + 1) * SUB, z]
                yp[r, h, ORIGIN - SUB:ORIGIN] = jnp.broadcast_to(u[x + r, 0:1, z], (SUB, LANES))
                top = jnp.broadcast_to(u[x + r, ny - 1:ny, z], (SUB, LANES))
                yp[r, h, ORIGIN + ny:ORIGIN + ny + SUB] = top
                yp[r, h, PAD - SUB + ny:PAD + ny] = top
                ycol = lambda o: yp[r, h, o:o + SUB]
                here = [w.at[r, h] for w in ywork]
                column_weights(ycol, here, ny)
                for tile in range(tiles):
                    m, p = column_part(ycol, here, tile)
                    at = (1, x + r, slice(tile * SUB, (tile + 1) * SUB), z)
                    to = (r, h, slice(tile * SUB, (tile + 1) * SUB))
                    ya[to] = fp[at] * p + fm[at] * m
                    yb[to] = gain[at] * (p + m)

    def back(slot):
        _, zm, zd, _, _, tm, td = slot
        for h in range(halves):
            tm[h] = zm[h * LANES:(h + 1) * LANES].T
            td[h] = zd[h * LANES:(h + 1) * LANES].T

    def total(i, slot):
        _, _, _, ya, yb, tm, td = slot
        x = 2 * i
        for h in range(halves):
            for r in range(2):
                for tile in range(tiles):
                    o = r * ny + tile * SUB
                    m, p = tm[h, o:o + SUB], td[h, o:o + SUB]
                    at = (x + r, slice(tile * SUB, (tile + 1) * SUB), slice(h * LANES, (h + 1) * LANES))
                    of = (2, first + x + r) + at[1:]
                    to = (r, h, slice(tile * SUB, (tile + 1) * SUB))
                    ac[at] = ya[to] + (fp[of] * p + fm[of] * m)
                    bb[at] = yb[to] + gain[of] * (p + m)

    forward(0, slots[0])

    def body(j, _):
        forward(2 * j + 1, slots[1])
        work(2 * j, slots[0])
        back(slots[0])
        total(2 * j, slots[0])
        forward(jnp.minimum(2 * j + 2, pairs - 1), slots[0])
        work(2 * j + 1, slots[1])
        back(slots[1])
        total(2 * j + 1, slots[1])
        return 0

    lax.fori_loop(0, pairs // 2, body, 0)


def parity():
    return lax.rem(lax.axis_index("gx"), 2)


def first_slab():
    return lax.axis_index("gx") == 0


def last_slab():
    return lax.axis_index("gx") == lax.axis_size("gx") - 1


def call(kernel, ins, outs, scratch, args, us):
    return pl.pallas_call(
        kernel,
        in_specs=ins,
        out_specs=[s for s, _ in outs],
        out_shape=[(pltpu.VMEM(shape, F32) if s is VM else jax.ShapeDtypeStruct(shape, F32)) for s, shape in outs],
        scratch_shapes=scratch,
        cost_estimate=pl.CostEstimate(flops=int(us * 1.15e9), bytes_accessed=0, transcendentals=0),
        compiler_params=pltpu.CompilerParams(vmem_limit_bytes=LIMIT),
    )(*args)


def send_rows(u, odd, near, far):
    last = u.shape[0] - 3

    def body(r, _):
        if near is not None:
            near[r] = u[(1 - odd) * last + r]
        if far is not None:
            far[r] = u[odd * last + r]
        return 0

    lax.fori_loop(0, 3, body, 0)


def prep_kernel(chunk, value, drift, gain, fp, fm, gv, vv, far, top, dv, sems, gsems, vsem):
    rows, ny, nz = value.shape
    n = rows // chunk
    moves = []
    for i in range(n):
        at = pl.ds(i * chunk, chunk)
        a = pltpu.make_async_copy(drift.at[:, at], dv.at[:, at], sems.at[i])
        b = pltpu.make_async_copy(gain.at[:, at], gv.at[:, at], gsems.at[i])
        a.start()
        b.start()
        moves.append((a, b))
    keep = pltpu.make_async_copy(value, vv, vsem.at[0])
    keep.start()
    best = jnp.zeros((SUB, LANES), F32)
    for i in range(n):
        moves[i][0].wait()
        moves[i][1].wait()

        def body(j, best):
            x = i * chunk + j // (ny // SUB)
            y = pl.multiple_of((j % (ny // SUB)) * SUB, SUB)
            for h in range(nz // LANES):
                at = (x, pl.ds(y, SUB), slice(h * LANES, (h + 1) * LANES))
                speed = None
                for k in range(3):
                    a = dv[(k,) + at]
                    w = jnp.abs(a) + jnp.abs(gv[(k,) + at])
                    fp[(k,) + at] = a - w
                    fm[(k,) + at] = a + w
                    speed = w if speed is None else speed + w
                best = jnp.maximum(best, speed)
            return best

        best = lax.fori_loop(0, chunk * (ny // SUB), body, best, unroll=4)
    top[...] = best
    keep.wait()
    send_rows(vv, parity(), None, far)


def yz_bounds_kernel(first, last, u, fp, fm, gain, dep, target, obstacle, ac, bb, done, lo, hi, tv, ov, sems, *scratch):
    a = pltpu.make_async_copy(target, tv, sems.at[0])
    b = pltpu.make_async_copy(obstacle, ov, sems.at[1])
    a.start()
    b.start()
    yz_pass(u, (fp, fm, gain), ac, bb, scratch, first, last)
    done[...] = jnp.zeros_like(done)
    a.wait()
    b.wait()

    def body(x, _):
        lo[x] = jnp.where(ov[x] == 1, 1.0, -jnp.inf)
        hi[x] = jnp.where(tv[x] == 1, -1.0, jnp.inf)
        return 0

    lax.fori_loop(0, u.shape[0], body, 0)


def yz_send_kernel(first, last, u, fp, fm, gain, dep, ac, bb, done, near, *scratch):
    send_rows(u, parity(), near, None)
    yz_pass(u, (fp, fm, gain), ac, bb, scratch, first, last)
    done[...] = jnp.zeros_like(done)


def yz_kernel(first, last, u, fp, fm, gain, dep, ac, bb, done, *scratch):
    yz_pass(u, (fp, fm, gain), ac, bb, scratch, first, last)
    done[...] = jnp.zeros_like(done)


def x_all(u, near, far, fields, ac, bb, span, finish, after=None):
    rows, ny, nz = u.shape
    odd = parity() == 1
    fp, fm, gain = fields

    def load(r, y, z):
        at = (pl.ds(y, SUB), pl.ds(z, LANES))
        if r < 3:
            got = jnp.where(odd, near[(r,) + at], far[(r,) + at])
            return jnp.where(first_slab(), u[(0,) + at], got)
        if r >= rows + 3:
            r -= rows + 3
            got = jnp.where(odd, far[(r,) + at], near[(r,) + at])
            return jnp.where(last_slab(), u[(rows - 1,) + at], got)
        return u[(r - 3,) + at]

    size = ac[0].shape[0]

    def part(parts, x, at):
        return parts[0][(x,) + at] if x < size else parts[1][(x - size,) + at]

    def sums(x, y, z, dm, dp):
        at = (x, pl.ds(y, SUB), pl.ds(z, LANES))
        a = part(ac, x, at[1:]) + fp[(0,) + at] * dp + fm[(0,) + at] * dm
        b = part(bb, x, at[1:]) + gain[(0,) + at] * (dp + dm)
        finish(x, y, z, a + jnp.abs(b))

    x_pass(load, rows, span, nz, sums, after)


def rate_x_kernel(u, near, far, fp, fm, gain, ac0, bb0, ac1, bb1, dep, total, done):
    done[...] = jnp.zeros_like(done)

    def finish(x, y, z, s):
        total[x, pl.ds(y, SUB), pl.ds(z, LANES)] = s

    x_all(u, near, far, (fp, fm, gain), (ac0, ac1), (bb0, bb1), (0, u.shape[1]), finish)


def first_kernel(mine, other, value, total, lo, hi, u, kappa, near, far):
    best = jnp.maximum(mine[...], other[...])
    best = jnp.max(jnp.max(best, axis=0, keepdims=True), axis=1, keepdims=True)
    k = jnp.broadcast_to(0.5 / best / 12.0, (SUB, LANES))
    kappa[...] = k
    rows, ny, nz = value.shape

    def body(x, _):
        for y in range(0, ny, SUB):
            for z in range(0, nz, LANES):
                at = (x, slice(y, y + SUB), slice(z, z + LANES))
                new = value[at] - k * total[at]
                u[at] = jnp.minimum(jnp.maximum(new, lo[at]), hi[at])
        return 0

    lax.fori_loop(0, rows, body, 0)
    send_rows(u, parity(), near, far)


def updater(weights, kappa, value, u, lo, hi, out):
    keep, take = weights

    def finish(x, y, z, total):
        at = (x, pl.ds(y, SUB), pl.ds(z, LANES))
        new = keep * value[at] + take * u[at] - (take * kappa[...]) * total
        out[at] = jnp.minimum(jnp.maximum(new, lo[at]), hi[at])
    return finish


def second_kernel(weights, u, near, far, kappa, value, fp, fm, gain, lo, hi, ac, bb, out, near_out, far_out):
    _, ny, nz = u.shape
    x_all(u, near, far, (fp, fm, gain), (ac,), (bb,), (0, ny), updater(weights, kappa, value, u, lo, hi, out))
    send_rows(out, parity(), near_out, far_out)


def third_kernel(weights, u, near, far, kappa, value, fp, fm, gain, lo, hi, ac, bb, out, keep, sems):
    _, ny, nz = u.shape

    def move(i, y):
        at = pl.ds(y, SUB)
        return pltpu.make_async_copy(keep.at[:, at], out.at[:, at], sems.at[i])

    x_all(u, near, far, (fp, fm, gain), (ac,), (bb,), (0, ny), updater(weights, kappa, value, u, lo, hi, keep),
          lambda i, y: move(i, y).start())

    def wait(i, _):
        move(i, pl.multiple_of(i * SUB, SUB)).wait()
        return 0

    lax.fori_loop(0, ny // SUB, wait, 0)


def shards(value, drift, gain, target, obstacle):
    count = lax.axis_size("gx")
    value, drift, gain, target, obstacle = (
        pltpu.with_memory_space_constraint(a, pltpu.HBM) for a in (value, drift, gain, target, obstacle))
    rows, ny, nz = value.shape
    flat, deep, tile = (rows, ny, nz), (3, rows, ny, nz), (SUB, LANES)
    ends = (3, ny, nz)
    pairs = [(i, i ^ 1) for i in range(count)]

    links = [(i, (i + 1) % count) for i in range(1, count, 2)]
    links += [(b, a) for a, b in links]
    chips = count // 2
    order = list(range(0, chips, 2)) + list(range(chips - 1 - chips % 2, 0, -2))

    def ring(reach):
        out = [(2 * order[i] + 1, 2 * order[(i + reach) % chips]) for i in range(chips)]
        return out + [(b, a) for a, b in out]

    def swap(x, perm):
        return lax.ppermute(x, "gx", perm)

    chunk = 2
    dma = pltpu.SemaphoreType.DMA
    fp, fm, gv, vv, far, top = call(
        functools.partial(prep_kernel, chunk),
        [HBM, HBM, HBM],
        [(VM, deep)] * 3 + [(VM, flat), (VM, ends), (VM, tile)],
        [pltpu.VMEM(deep, F32)] + [dma((rows // chunk,))] * 2 + [dma((1,))],
        (value, drift, gain), 3)
    fields = (fp, fm, gv)
    work = yz_scratch(ny, nz)
    other = swap(top, pairs)
    far = swap(far, links)

    def join(top, other, done):
        return jnp.maximum(jnp.maximum(top, other), done)

    def rate_yz(u, first, last, dep, us):
        part = (last - first, ny, nz)
        return call(functools.partial(yz_kernel, first, last), [VM] * 4 + [ANY],
                    [(VM, part)] * 2 + [(VM, tile)], work, (u,) + fields + (dep,), us)

    mid = 2 * (3 * rows // 8)
    top = jnp.maximum(top, other)
    other = swap(top, ring(1))
    ac0, bb0, done, lo, hi = call(
        functools.partial(yz_bounds_kernel, 0, mid), [VM] * 4 + [ANY, HBM, HBM],
        [(VM, (mid, ny, nz))] * 2 + [(VM, tile)] + [(VM, flat)] * 2,
        [pltpu.VMEM(flat, jnp.int32)] * 2 + [dma((2,))] + work, (vv,) + fields + (top, target, obstacle), 4)
    top = join(top, other, done)
    other = swap(top, pairs)
    ac1, bb1, done, near = call(
        functools.partial(yz_send_kernel, mid, rows), [VM] * 4 + [ANY],
        [(VM, (rows - mid, ny, nz))] * 2 + [(VM, tile), (VM, ends)], work, (vv,) + fields + (top,), 1.5)
    near = swap(near, pairs)
    top = join(top, other, done)
    reach = 3
    other = swap(top, ring(reach))
    total, done = call(
        rate_x_kernel, [VM] * 10 + [ANY], [(VM, flat), (VM, tile)], [],
        (vv, near, far) + fields + (ac0, bb0, ac1, bb1, top), 2.4)
    top = join(top, other, done)
    other = swap(top, pairs)
    while 3 * reach < count // 2:
        reach *= 3
        top = jnp.maximum(top, other)
        top = jnp.maximum(top, swap(top, ring(reach)))
        other = swap(top, pairs)
    u, kappa, near, far = call(
        first_kernel, [VM] * 6, [(VM, flat), (VM, tile), (VM, ends), (VM, ends)], [],
        (top, other, vv, total, lo, hi), 1)
    for i, weights in enumerate(((0.75, 0.25), (1 / 3, 2 / 3))):
        far = swap(far, links)
        near = swap(near, pairs)
        ac, bb, _ = rate_yz(u, 0, rows, kappa, 6)
        args = (u, near, far, kappa, vv) + fields + (lo, hi, ac, bb)
        if i == 0:
            u, near, far = call(
                functools.partial(second_kernel, weights), [VM] * 12,
                [(VM, flat), (VM, ends), (VM, ends)], [], args, 3)
        else:
            return call(
                functools.partial(third_kernel, weights), [VM] * 12,
                [(ANY, flat)], [pltpu.VMEM(flat, F32), dma((ny // SUB,))], args, 3)[0]


def solution(mesh):
    flat = P(("group", "gx"), None, None)
    deep = P(None, ("group", "gx"), None, None)
    return jax.shard_map(
        shards,
        mesh=mesh,
        in_specs=(flat, deep, deep, flat, flat),
        out_specs=flat,
        check_vma=False,
    )
```
